32 devices in a mesh: gx: 16 (over z, y, core), gy: 2 (over x).
Axes of the slice: x: 2, y: 2, z: 4, core: 2. Of those that a mesh axis runs over, the one named last changes fastest.
Arguments:
- features: bfloat16 [16, 2, 3, 512, 192], P('gx', 'gy'), may hold values from -6 to 6
- weight: bfloat16 [5184, 192], replicated, may hold values from -0.078125 to 0.078125
- cotangent: bfloat16 [16, 2, 3, 64, 192], P('gx', 'gy'), may hold values from -6 to 6
- valid: int32 [16, 2, 3], P('gx', 'gy'), may hold values from 0 to 1, as said below
- local_rules: int32 [16, 2, 2, 12], P('gx', 'gy'), may hold values from 0 to 3, as said below
- local_codes: int32 [16, 2, 12], P('gx', 'gy'), may hold values from 0 to 7
- remote_rules: int32 [16, 2, 2, 3, 3], P('gx', 'gy'), may hold values from 0 to 3, as said below
- remote_codes: int32 [16, 2, 3, 3], P('gx', 'gy'), may hold values from 1 to 7, as said below
Outputs:
- output: bfloat16 [16, 2, 3, 64, 192], P('gx', 'gy')
- features_grad: bfloat16 [16, 2, 3, 512, 192], P('gx', 'gy')
- weight_grad: float32 [5184, 192], P('gx')
The draws below stay inside these ranges and needn't reach their ends.
Inputs may be any that keep to these rules, and one draw needn't show every extreme that they name: `valid`: 1 marks a live brick slot; on each device the live slots come first and at least one slot is live. `local_rules`: entry [., ., 0, e] is a source slot and [., ., 1, e] a target slot of the same device; a target 3 marks an empty entry; non-empty entries name live slots. `remote_rules`: class m (third dimension) entry: a source slot on this device and a target slot on the device one step higher along gx (m = 0), along gy (m = 1) or along both (m = 2); a target 3 marks an empty entry; non-empty entries name live slots; devices at the upper end of an axis have no non-empty entries in the classes that cross it. `remote_codes`: the offset k mod 2 is 1 in classes 0 and 2, and the offset (k // 2) mod 2 is 1 in classes 1 and 2.
All inputs are finite; a program needn't handle non-finite values.
Results may differ from the reference program's by a relative error of at most 0.0045.
Values may be sent and summed in bfloat16 or wider, within the bound.
A program may use at most 128 MiB of HBM per device.

```python
import jax
import jax.numpy as jnp
import numpy as np
from jax import lax

C = 192
NB = 3
RL = 12
RR = 3
GRID_X = 16
GRID_Y = 2


def live_counts(key):
    return jax.random.randint(jax.random.fold_in(key, 11), (GRID_X, GRID_Y), 1, NB + 1)


def draw_valid(key, part):
    live_count = live_counts(key)
    slot_ids = jnp.arange(NB, dtype=jnp.int32)[None, None, :]
    return (slot_ids < live_count[..., None]).astype(jnp.int32)


def local_plan(key):
    live_count = live_counts(key)
    slot_ids = jnp.broadcast_to(jnp.arange(RL, dtype=jnp.int32)[None, None, :], (GRID_X, GRID_Y, RL))
    own_slot = slot_ids < NB
    extra_count = jax.random.randint(jax.random.fold_in(key, 21), (GRID_X, GRID_Y), NB, 3 * NB)
    extra_live = (slot_ids >= NB) & (slot_ids < NB + extra_count[..., None])
    random_source = jax.random.randint(jax.random.fold_in(key, 22), (GRID_X, GRID_Y, RL), 0, live_count[..., None])
    random_target = jax.random.randint(jax.random.fold_in(key, 23), (GRID_X, GRID_Y, RL), 0, live_count[..., None])
    own_live = own_slot & (slot_ids < live_count[..., None])
    source = jnp.where(own_slot, slot_ids, jnp.where(extra_live, random_source, 0))
    target = jnp.where(own_live, slot_ids, jnp.where(extra_live, random_target, NB))
    code_list = jnp.where(own_slot, 0, jax.random.randint(jax.random.fold_in(key, 24), (GRID_X, GRID_Y, RL), 1, 8))
    return (jnp.stack([source, target], axis=2).astype(jnp.int32), code_list.astype(jnp.int32))


def draw_local_rules(key, part):
    return local_plan(key)[0]


def draw_local_codes(key, part):
    return local_plan(key)[1]


def remote_plan(key):
    live_count = live_counts(key)
    above_x = jnp.roll(live_count, -1, axis=0)
    above_y = jnp.roll(live_count, -1, axis=1)
    above_both = jnp.roll(above_x, -1, axis=1)
    dest_live = jnp.stack([above_x, above_y, above_both], axis=2)
    lower_x = jnp.broadcast_to(jnp.arange(GRID_X)[:, None] < GRID_X - 1, (GRID_X, GRID_Y))
    lower_y = jnp.broadcast_to(jnp.arange(GRID_Y)[None, :] < GRID_Y - 1, (GRID_X, GRID_Y))
    reach = jnp.stack([lower_x, lower_y, lower_x & lower_y], axis=2).astype(jnp.int32)
    rule_count = jax.random.randint(jax.random.fold_in(key, 31), (GRID_X, GRID_Y, 3), 1, RR + 1) * reach
    slot_ids = jnp.arange(RR, dtype=jnp.int32)[None, None, None, :]
    live_rule = slot_ids < rule_count[..., None]
    shape_all = (GRID_X, GRID_Y, 3, RR)
    random_source = jax.random.randint(jax.random.fold_in(key, 32), shape_all, 0, live_count[..., None, None])
    random_target = jax.random.randint(jax.random.fold_in(key, 33), shape_all, 0, dest_live[..., None])
    source = jnp.where(live_rule, random_source, 0)
    target = jnp.where(live_rule, random_target, NB)
    free_x = jax.random.randint(jax.random.fold_in(key, 34), shape_all, 0, 2)
    free_y = jax.random.randint(jax.random.fold_in(key, 35), shape_all, 0, 2)
    free_z = jax.random.randint(jax.random.fold_in(key, 36), shape_all, 0, 2)
    class_ids = jnp.arange(3, dtype=jnp.int32)[None, None, :, None]
    offset_x = jnp.where(class_ids == 1, free_x, 1)
    offset_y = jnp.where(class_ids == 0, free_y, 1)
    code_list = offset_x + 2 * offset_y + 4 * free_z
    return (jnp.stack([source, target], axis=2).astype(jnp.int32), code_list.astype(jnp.int32))


def draw_remote_rules(key, part):
    return remote_plan(key)[0]


def draw_remote_codes(key, part):
    return remote_plan(key)[1]


def levels(own_key, shape, cuts, smallest, largest):
    gain = 1.0
    for dim, parts in cuts:
        heights = jax.random.uniform(jax.random.fold_in(jax.random.fold_in(own_key, 6), dim), (parts,), jnp.float32, smallest / len(cuts), largest / len(cuts))
        gain = gain * jnp.repeat(jnp.exp(heights), shape[dim] // parts).reshape((-1,) + (1,) * (len(shape) - 1 - dim))
    return gain


def noise(own_key, dims, deviation, limit, shards=(), held_as=jnp.bfloat16):
    factor_of = levels(own_key, dims, shards, -0.22, 0.18) if shards else 1.0
    array = jax.random.normal(own_key, dims, jnp.float32) * deviation * factor_of
    return jnp.minimum(jnp.maximum(array, -limit), limit).astype(held_as)


def setup_inputs(seed: int = 0) -> dict:
    streams_of = jax.random.split(jax.random.key(seed), 9)
    features = noise(streams_of[0], (GRID_X, GRID_Y, NB, 512, C), 1.0, 6.0, ((0, 16), (1, 2)))
    weight = noise(streams_of[1], (27 * C, C), (27 * C) ** -0.5, 0.078125)
    cotangent = noise(streams_of[2], (GRID_X, GRID_Y, NB, 64, C), 1.0, 6.0, ((0, 16), (1, 2)))
    valid = draw_valid(jax.random.fold_in(streams_of[8], 71), 0)
    local_rules = draw_local_rules(jax.random.fold_in(streams_of[8], 71), 0)
    local_codes = draw_local_codes(jax.random.fold_in(streams_of[8], 71), 0)
    remote_rules = draw_remote_rules(jax.random.fold_in(streams_of[8], 71), 0)
    remote_codes = draw_remote_codes(jax.random.fold_in(streams_of[8], 71), 0)
    return {"features": features, "weight": weight, "cotangent": cotangent, "valid": valid, "local_rules": local_rules, "local_codes": local_codes, "remote_rules": remote_rules, "remote_codes": remote_codes}


def offset_table(row_x, row_y, row_z):
    code_list = np.arange(8)[:, None]
    step_x = code_list % 2
    step_y = (code_list // 2) % 2
    step_z = code_list // 4
    inside = ((step_x == 0) | (row_x[None, :] == 0)) & ((step_y == 0) | (row_y[None, :] == 0)) & ((step_z == 0) | (row_z[None, :] == 0))
    source_row = (row_x[None, :] + 4 * step_x) * 25 + (row_y[None, :] + 4 * step_y) * 5 + row_z[None, :] + 4 * step_z
    return np.where(inside, source_row, 125).astype(np.int32)


def full_table():
    voxel_ids = np.arange(64)
    return offset_table(voxel_ids // 16, (voxel_ids // 4) % 4, voxel_ids % 4)


def brick_patches(one_brick):
    channels = one_brick.shape[-1]
    cube = one_brick.reshape(8, 8, 8, channels)
    padded = jnp.pad(cube, ((1, 2), (1, 2), (1, 2), (0, 0)))
    tap_list = []
    for along_x in range(3):
        for along_y in range(3):
            for along_z in range(3):
                tap_list.append(padded[along_x:along_x + 9:2, along_y:along_y + 9:2, along_z:along_z + 9:2, :])
    return jnp.stack(tap_list, axis=3).reshape(125, 27 * channels)


def brick_fold(patch_grads, channels):
    tap_grads = patch_grads.reshape(5, 5, 5, 27, channels)
    padded = jnp.zeros((11, 11, 11, channels), jnp.float32)
    tap_index = 0
    for along_x in range(3):
        for along_y in range(3):
            for along_z in range(3):
                padded = padded.at[along_x:along_x + 9:2, along_y:along_y + 9:2, along_z:along_z + 9:2, :].add(tap_grads[:, :, :, tap_index, :])
                tap_index = tap_index + 1
    return padded[1:9, 1:9, 1:9, :].reshape(512, channels)


def reference(features, weight, cotangent, valid, local_rules, local_codes, remote_rules, remote_codes):
    channels = features.shape[-1]
    live_mask = valid.astype(jnp.bfloat16)[..., None, None]
    live_float = valid.astype(jnp.float32)[..., None, None]
    masked = features * live_mask
    tile_bricks = masked.reshape(GRID_X * GRID_Y, NB, 512, channels)

    def forward_tile(tile):
        patches = jax.vmap(brick_patches)(tile).reshape(NB * 125, 27 * channels)
        return jnp.dot(patches, weight, preferred_element_type=jnp.float32).reshape(NB, 125, channels)

    partials = lax.map(forward_tile, tile_bricks).reshape(GRID_X * GRID_Y * NB, 125, channels)
    zero_rows = jnp.zeros((partials.shape[0], 1, channels), jnp.float32)
    padded = jnp.concatenate([partials, zero_rows], axis=1).reshape(GRID_X, GRID_Y, NB, 126, channels)
    full_map = jnp.asarray(full_table())
    column_x = jnp.arange(GRID_X, dtype=jnp.int32)[:, None, None]
    column_y = jnp.arange(GRID_Y, dtype=jnp.int32)[None, :, None]
    rule_sets = [(local_rules[:, :, 0], local_rules[:, :, 1], local_codes, 0, 0)]
    for rule_class, steps_xy in enumerate(((1, 0), (0, 1), (1, 1))):
        rule_sets.append((remote_rules[:, :, 0, rule_class], remote_rules[:, :, 1, rule_class], remote_codes[:, :, rule_class], steps_xy[0], steps_xy[1]))
    totals = jnp.zeros((GRID_X, GRID_Y, NB + 1, 64, channels), jnp.float32)
    placed = []
    for sources, targets, code_list, step_x, step_y in rule_sets:
        dest_x = jnp.broadcast_to(column_x + step_x, sources.shape)
        dest_y = jnp.broadcast_to(column_y + step_y, sources.shape)
        inside = (dest_x < GRID_X) & (dest_y < GRID_Y)
        kept_target = jnp.where(inside, targets, NB).astype(jnp.int32)
        dest_x = jnp.minimum(dest_x, GRID_X - 1).astype(jnp.int32)
        dest_y = jnp.minimum(dest_y, GRID_Y - 1).astype(jnp.int32)
        row_index = full_map[code_list]
        anchor_x = jnp.broadcast_to(column_x, sources.shape)[..., None]
        anchor_y = jnp.broadcast_to(column_y, sources.shape)[..., None]
        pieces = padded[anchor_x, anchor_y, sources[..., None], row_index]
        totals = totals.at[dest_x, dest_y, kept_target].add(pieces)
        placed.append((anchor_x, anchor_y, sources, row_index, dest_x, dest_y, kept_target))
    output = (totals[:, :, :NB] * live_float).astype(jnp.bfloat16)

    grad_out = (cotangent * live_mask).astype(jnp.float32)
    grad_pad = jnp.concatenate([grad_out, jnp.zeros((GRID_X, GRID_Y, 1, 64, channels), jnp.float32)], axis=2)
    grad_rows = jnp.zeros((GRID_X, GRID_Y, NB, 126, channels), jnp.float32)
    for anchor_x, anchor_y, sources, row_index, dest_x, dest_y, kept_target in placed:
        grad_rows = grad_rows.at[anchor_x, anchor_y, sources[..., None], row_index].add(grad_pad[dest_x, dest_y, kept_target])
    grad_rounded = grad_rows[:, :, :, :125].astype(jnp.bfloat16).reshape(GRID_X * GRID_Y, NB * 125, channels)

    def fold_one(patch_grads):
        return brick_fold(patch_grads, channels)

    def backward_tile(running, inputs):
        tile, tile_grads = inputs
        patches = jax.vmap(brick_patches)(tile).reshape(NB * 125, 27 * channels)
        patch_grads = jnp.dot(tile_grads, weight.T, preferred_element_type=jnp.float32).reshape(NB, 125, 27 * channels)
        running = running + jnp.dot(patches.T, tile_grads, preferred_element_type=jnp.float32)
        return running, jax.vmap(fold_one)(patch_grads)

    weight_grad, folded = lax.scan(backward_tile, jnp.zeros((27 * channels, channels), jnp.float32), (tile_bricks, grad_rounded))
    features_grad = (folded.reshape(GRID_X, GRID_Y, NB, 512, channels) * live_float).astype(jnp.bfloat16)
    return output, features_grad, weight_grad
```

```python
import jax
import jax.numpy as jnp
import numpy as np
from jax import lax
from jax.experimental import pallas as pl
from jax.experimental.pallas import tpu as pltpu
from jax.sharding import PartitionSpec as P

BF = jnp.bfloat16
F32 = jnp.float32
MESH = pl.DeviceIdType.MESH

PAIRS = [(d, k) for d in range(8) for k in range(8) if k & ~d == 0]
PAIR_AT = {pair: at for at, pair in enumerate(PAIRS)}


def tap_list():
    taps = []
    for e in range(3):
        for f in range(3):
            for g in range(3):
                cls = (e != 1) + 2 * (f != 1) + 4 * (g != 1)
                shift = (e == 0) + 2 * (f == 0) + 4 * (g == 0)
                taps.append((9 * e + 3 * f + g, int(cls), int(shift)))
    return taps


TAPS = tap_list()


def bits(k):
    return k % 2, k // 2 % 2, k // 4


def rule_blocks(bricks):
    v = np.arange(64)
    coords = [v // 16, v // 4 % 4, v % 4]
    face = np.concatenate([v, (np.arange(16) // 4) * 16 + np.arange(16) % 4])
    blocks = []
    for d, k in PAIRS:
        hit = np.ones((64, 64), bool)
        for axis in range(3):
            row = coords[axis][:, None] + 4 * bits(k)[axis]
            col = coords[axis][None, :] + bits(d)[axis]
            hit &= row == col
        blocks.append(np.tile(hit[face], (1, bricks)))
    return np.stack(blocks).astype(np.float32)


def parity_order():
    rows = np.zeros(512, np.int64)
    for cls in range(8):
        px, py, pz = bits(cls)
        for v in range(64):
            a, b, c = v // 16, v // 4 % 4, v % 4
            rows[cls * 64 + v] = (2 * a + px) * 64 + (2 * b + py) * 8 + 2 * c + pz
    return rows


def face_picks(bricks):
    picks = np.zeros((3, bricks * 16, bricks * 64), np.float32)
    for t in range(bricks):
        for v in range(16):
            picks[0, t * 16 + v, t * 64 + v] = 1
            picks[1, t * 16 + v, t * 64 + (v // 4) * 16 + v % 4] = 1
            picks[2, t * 16 + v, t * 64 + v] = 1
    return picks.reshape(3 * bricks * 16, bricks * 64)


def chunks_of(rows, count):
    units = rows // 16
    cuts = [round(units * q / count) * 16 for q in range(count + 1)]
    return [(lo, hi - lo) for lo, hi in zip(cuts[:-1], cuts[1:])]


def dot(a, b):
    return jnp.dot(a, b, preferred_element_type=F32)


def dot_nt(a, b):
    return lax.dot_general(a, b, (((1,), (1,)), ((), ())), preferred_element_type=F32)


def dot_tn(a, b):
    return lax.dot_general(a, b, (((0,), (0,)), ((), ())), preferred_element_type=F32)


def make_kernel(ngx, ngy, bricks, local_count, remote_count, channels, chunk_count):
    rows = bricks * 64
    frows = bricks * 16
    share = 27 * channels // ngx
    padded = -(-share // 16) * 16
    chips = ngx // 2
    outer = ngx // 4
    chunks = chunks_of(padded, chunk_count)
    nq = len(chunks)
    ext = rows + 3 * frows

    def kernel(
        valid, lrules, lcodes, rrules, rcodes,
        feat, weight, cot, blocks, perm, perm_t, picks, picks_t, slot_of, eye,
        out, fgrad, wgrad,
        x_ref, xt_ref, m_ref, g_ref, t_ref, ge, gface, frecv, fsend, totals, fcls,
        wg, buf, recv_a, acc, recv_b, acc2, recv_c, final,
        s_g, r_g, s_f, r_f, s_a, r_a, s_b, r_b, s_c, r_c, s_d, r_d,
    ):
        i = lax.axis_index("gx")
        j = lax.axis_index("gy")
        core = lax.rem(i, 2)
        inner = lax.rem(i // 2, 2)
        z = i // 4
        up_i, dn_i = lax.rem(i + 1, ngx), lax.rem(i + ngx - 1, ngx)
        up_j, dn_j = lax.rem(j + 1, ngy), lax.rem(j + ngy - 1, ngy)
        ups = [(up_i, j), (i, up_j), (up_i, up_j)]
        downs = [(dn_i, j), (i, dn_j), (dn_i, dn_j)]
        core_peer = (i + 1 - 2 * core, j)
        inner_peer = (i + 2 - 4 * inner, j)
        outer_peers = [(lax.rem(i + 4 * k, ngx), j) for k in range(1, outer)]
        gy_peers = [(i, lax.rem(j + k, ngy)) for k in range(1, ngy)]
        peers = ups + downs + [core_peer, inner_peer] + outer_peers + gy_peers

        barrier = pltpu.get_barrier_semaphore()
        for peer in peers:
            pl.semaphore_signal(barrier, inc=1, device_id=peer, device_id_type=MESH)

        live = [valid[0, 0, s] for s in range(bricks)]
        live_f = [v.astype(F32) for v in live]
        for s in range(bricks):
            ge[s * 64 : (s + 1) * 64] = (cot[0, 0, s].astype(F32) * live_f[s]).astype(BF)
        own = ge[0:rows]
        gface[...] = dot(picks[0 : 2 * frows], own).astype(BF)
        pl.semaphore_wait(barrier, len(peers))

        def remote(src, dst, ssem, rsem, peer):
            return pltpu.make_async_remote_copy(
                src_ref=src, dst_ref=dst, send_sem=ssem, recv_sem=rsem,
                device_id=peer, device_id_type=MESH,
            )

        face_copies = []
        for c in range(3):
            src = gface.at[pl.ds(frows * (c % 2), frows)]
            dst = ge.at[pl.ds(rows + c * frows, frows)]
            copy = remote(src, dst, s_g.at[c], r_g.at[c], downs[c])
            copy.start()
            face_copies.append(copy)

        for s in range(bricks):
            moved = dot(perm[...], feat[0, 0, s]) * live_f[s]
            for cls in range(8):
                x_ref[cls, s * 64 : (s + 1) * 64] = moved[cls * 64 : (cls + 1) * 64].astype(BF)
        for cls in range(8):
            xt_ref[cls] = dot_nt(eye[...], x_ref[cls]).astype(BF)

        groups = 8 * bricks
        row_id = lax.broadcasted_iota(jnp.int32, (4 * groups, 128), 0)
        lane_id = lax.broadcasted_iota(jnp.int32, (4 * groups, 128), 1)
        counts = jnp.zeros((4 * groups, 128), F32)

        def count(total, kind, source, target, code):
            at = jnp.where(target < bricks, kind * groups + 8 * target + code, -1)
            return total + jnp.where((row_id == at) & (lane_id == source), 1.0, 0.0)

        for e in range(local_count):
            counts = count(counts, 0, lrules[0, 0, 0, e], lrules[0, 0, 1, e], lcodes[0, 0, e])
        for c in range(3):
            for e in range(remote_count):
                counts = count(
                    counts, c + 1, rrules[0, 0, 0, c, e], rrules[0, 0, 1, c, e], rcodes[0, 0, c, e]
                )
        spread = dot(counts.astype(BF), slot_of[...])

        for d in range(8):
            codes = [k for k in range(8) if k & ~d == 0]
            full = {k: blocks[PAIR_AT[(d, k)]].astype(F32) for k in codes}
            for kind in range(4):
                need = (0, 1, 2, 3)[kind]
                lo, hi = ((0, 64), (0, 16), (64, 80), (0, 16))[kind]
                for t in range(bricks):
                    total = jnp.zeros((hi - lo, rows), F32)
                    for k in codes:
                        if k & need == need:
                            at = kind * groups + 8 * t + k
                            total = total + spread[at : at + 1] * full[k][lo:hi]
                    first = t * 64 if kind == 0 else rows + (kind - 1) * frows + t * 16
                    m_ref[d, first : first + hi - lo] = total.astype(BF)

        for copy in face_copies:
            copy.wait()
        grads = ge[...]
        for d in range(8):
            g_ref[d] = dot_tn(m_ref[d], grads).astype(BF)

        a_copies = []
        built = 0
        for tap, cls, shift in TAPS:
            wg[tap * channels : (tap + 1) * channels] = dot(xt_ref[cls], g_ref[shift])
            while built < chips and 2 * share * (built + 1) <= (tap + 1) * channels:
                for h in range(2):
                    first = share * (2 * built + h)
                    block = wg[first : first + share].astype(BF)
                    if padded > share:
                        fill = jnp.zeros((padded - share, channels), BF)
                        block = jnp.concatenate([block, fill], axis=0)
                    buf[2 * built + h] = block
                copy = remote(
                    buf.at[2 * built + 1 - core], recv_a.at[built],
                    s_a.at[built], r_a.at[built], core_peer,
                )
                copy.start()
                a_copies.append(copy)
                built += 1

        for d in range(8):
            total = None
            for tap, cls, shift in TAPS:
                if shift == d:
                    term = dot(x_ref[cls], weight[tap * channels : (tap + 1) * channels])
                    total = term if total is None else total + term
            t_ref[d] = total

        for copy in a_copies:
            copy.wait_recv()
        b_copies = []
        for q, (lo, n) in enumerate(chunks):
            for m in range(chips):
                mine = buf[2 * m + core, lo : lo + n].astype(F32)
                acc[m % 2, m // 2, lo : lo + n] = (
                    mine + recv_a[m, lo : lo + n].astype(F32)
                ).astype(BF)
            copy = remote(
                acc.at[1 - inner, :, pl.ds(lo, n)], recv_b.at[:, pl.ds(lo, n)],
                s_b.at[q], r_b.at[q], inner_peer,
            )
            copy.start()
            b_copies.append(copy)

        total = None
        for d in range(8):
            value = t_ref[d]
            high = value.astype(BF)
            low = (value - high.astype(F32)).astype(BF)
            term = dot(m_ref[d], high) + dot(m_ref[d], low)
            total = term if total is None else total + term
        totals[...] = total[0:rows]
        fsend[...] = total[rows:ext].astype(BF)
        f_copies = []
        for c in range(3):
            span = pl.ds(c * frows, frows)
            copy = remote(fsend.at[span], frecv.at[span], s_f.at[c], r_f.at[c], ups[c])
            copy.start()
            f_copies.append(copy)

        def second(q):
            lo, n = chunks[q]
            b_copies[q].wait_recv()
            for o in range(outer):
                acc2[o, lo : lo + n] = (
                    acc[inner, o, lo : lo + n].astype(F32) + recv_b[o, lo : lo + n].astype(F32)
                ).astype(BF)
            started = []
            for k in range(1, outer):
                copy = remote(
                    acc2.at[lax.rem(z + k, outer), pl.ds(lo, n)], recv_c.at[k - 1, pl.ds(lo, n)],
                    s_c.at[q, k - 1], r_c.at[q, k - 1], outer_peers[k - 1],
                )
                copy.start()
                started.append(copy)
            return started

        def third(q):
            lo, n = chunks[q]
            total = acc2[z, lo : lo + n].astype(F32)
            for k in range(1, outer):
                c_copies[q][k - 1].wait_recv()
                total = total + recv_c[k - 1, lo : lo + n].astype(F32)
            final[j, lo : lo + n] = total.astype(BF)
            started = []
            for k in range(1, ngy):
                mine = final.at[j, pl.ds(lo, n)]
                copy = remote(mine, mine, s_d.at[q, k - 1], r_d.at[q, k - 1], gy_peers[k - 1])
                copy.start()
                started.append(copy)
            return started

        def feature_class(cls):
            total = None
            for tap, tap_cls, shift in TAPS:
                if tap_cls == cls:
                    term = dot_nt(g_ref[shift], weight[tap * channels : (tap + 1) * channels])
                    total = term if total is None else total + term
            for s in range(bricks):
                fcls[s, cls * 64 : (cls + 1) * 64] = (
                    total[s * 64 : (s + 1) * 64] * live_f[s]
                ).astype(BF)

        c_copies = []
        for cls in range(4):
            feature_class(cls)
        c_copies.append(second(0))
        for cls in range(4, 7):
            feature_class(cls)
        for q in range(1, nq):
            c_copies.append(second(q))
            if q == 1:
                feature_class(7)
        for s in range(bricks):
            fgrad[0, 0, s] = dot(perm_t[...], fcls[s]).astype(BF)

        for copy in f_copies:
            copy.wait()
        result = totals[...] + dot(picks_t[...], frecv[...])
        for s in range(bricks):
            out[0, 0, s] = (result[s * 64 : (s + 1) * 64] * live_f[s]).astype(BF)

        d_copies = [third(q) for q in range(nq)]
        for q, (lo, n) in enumerate(chunks):
            for copy in d_copies[q]:
                copy.wait_recv()
            total = final[0, lo : lo + n].astype(F32)
            for k in range(1, ngy):
                total = total + final[k, lo : lo + n].astype(F32)
            keep = min(n, share - lo)
            wgrad[lo : lo + keep] = total[0:keep]

        for copy in a_copies + b_copies:
            copy.wait_send()
        for copies in c_copies + d_copies:
            for copy in copies:
                copy.wait_send()

    dma = pltpu.SemaphoreType.DMA
    scratch = [
        pltpu.VMEM((8, rows, channels), BF),
        pltpu.VMEM((8, channels, rows), BF),
        pltpu.VMEM((8, ext, rows), BF),
        pltpu.VMEM((8, rows, channels), BF),
        pltpu.VMEM((8, rows, channels), F32),
        pltpu.VMEM((ext, channels), BF),
        pltpu.VMEM((2 * frows, channels), BF),
        pltpu.VMEM((3 * frows, channels), BF),
        pltpu.VMEM((3 * frows, channels), BF),
        pltpu.VMEM((rows, channels), F32),
        pltpu.VMEM((bricks, 512, channels), BF),
        pltpu.VMEM((27 * channels, channels), F32),
        pltpu.VMEM((ngx, padded, channels), BF),
        pltpu.VMEM((chips, padded, channels), BF),
        pltpu.VMEM((2, outer, padded, channels), BF),
        pltpu.VMEM((outer, padded, channels), BF),
        pltpu.VMEM((outer, padded, channels), BF),
        pltpu.VMEM((outer - 1, padded, channels), BF),
        pltpu.VMEM((ngy, padded, channels), BF),
        dma((3,)), dma((3,)), dma((3,)), dma((3,)),
        dma((chips,)), dma((chips,)), dma((nq,)), dma((nq,)),
        dma((nq, outer - 1)), dma((nq, outer - 1)),
        dma((nq, ngy - 1)), dma((nq, ngy - 1)),
    ]
    return kernel, scratch, share


def solution(mesh):
    ngx, ngy = mesh.shape["gx"], mesh.shape["gy"]

    def shards(
        features, weight, cotangent, valid, local_rules, local_codes, remote_rules, remote_codes
    ):
        bricks = features.shape[2]
        channels = features.shape[-1]
        local_count = local_codes.shape[-1]
        remote_count = remote_codes.shape[-1]
        kernel, scratch, share = make_kernel(
            ngx, ngy, bricks, local_count, remote_count, channels, 3
        )
        order = parity_order()
        perm = np.zeros((512, 512), np.float32)
        perm[np.arange(512), order] = 1
        picks = face_picks(bricks)
        slot_of = (np.arange(128)[:, None] == (np.arange(bricks * 64) // 64)[None, :]).astype(
            np.float32
        )
        consts = [
            jnp.asarray(c, BF)
            for c in (
                rule_blocks(bricks), perm, perm.T, picks, picks.T, slot_of,
                np.eye(channels, dtype=np.float32),
            )
        ]
        vmem = pl.BlockSpec(memory_space=pltpu.VMEM)
        smem = pl.BlockSpec(memory_space=pltpu.SMEM)
        return pl.pallas_call(
            kernel,
            out_shape=(
                jax.ShapeDtypeStruct(cotangent.shape, BF),
                jax.ShapeDtypeStruct(features.shape, BF),
                jax.ShapeDtypeStruct((share, channels), F32),
            ),
            in_specs=[smem] * 5 + [vmem] * 10,
            out_specs=(vmem, vmem, vmem),
            scratch_shapes=scratch,
            compiler_params=pltpu.CompilerParams(
                collective_id=0, has_side_effects=True, vmem_limit_bytes=56 * 1024 * 1024
            ),
        )(
            valid, local_rules, local_codes, remote_rules, remote_codes,
            features, weight, cotangent, *consts,
        )

    return jax.shard_map(
        shards,
        mesh=mesh,
        in_specs=(
            P("gx", "gy", None, None, None),
            P(),
            P("gx", "gy", None, None, None),
            P("gx", "gy", None),
            P("gx", "gy", None, None),
            P("gx", "gy", None),
            P("gx", "gy", None, None, None),
            P("gx", "gy", None, None),
        ),
        out_specs=(P("gx", "gy", None, None, None), P("gx", "gy", None, None, None), P("gx", None)),
        check_vma=False,
    )
```

```python
import jax
import jax.numpy as jnp
import numpy as np
from jax import lax
from jax.experimental import pallas as pl
from jax.experimental.pallas import tpu as pltpu
from jax.sharding import PartitionSpec as P

BF = jnp.bfloat16
F32 = jnp.float32
MESH = pl.DeviceIdType.MESH

PAIRS = [(d, k) for d in range(8) for k in range(8) if k & ~d == 0]
PAIR_AT = {pair: at for at, pair in enumerate(PAIRS)}


def tap_list():
    taps = []
    for e in range(3):
        for f in range(3):
            for g in range(3):
                cls = (e != 1) + 2 * (f != 1) + 4 * (g != 1)
                shift = (e == 0) + 2 * (f == 0) + 4 * (g == 0)
                taps.append((9 * e + 3 * f + g, int(cls), int(shift)))
    return taps


TAPS = tap_list()


def bits(k):
    return k % 2, k // 2 % 2, k // 4


def rule_blocks(bricks):
    v = np.arange(64)
    coords = [v // 16, v // 4 % 4, v % 4]
    face = np.concatenate([v, (np.arange(16) // 4) * 16 + np.arange(16) % 4])
    blocks = []
    for d, k in PAIRS:
        hit = np.ones((64, 64), bool)
        for axis in range(3):
            row = coords[axis][:, None] + 4 * bits(k)[axis]
            col = coords[axis][None, :] + bits(d)[axis]
            hit &= row == col
        blocks.append(np.tile(hit[face], (1, bricks)))
    return np.stack(blocks).astype(np.float32)


def parity_order():
    rows = np.zeros(512, np.int64)
    for cls in range(8):
        px, py, pz = bits(cls)
        for v in range(64):
            a, b, c = v // 16, v // 4 % 4, v % 4
            rows[cls * 64 + v] = (2 * a + px) * 64 + (2 * b + py) * 8 + 2 * c + pz
    return rows


def face_picks(bricks):
    picks = np.zeros((3, bricks * 16, bricks * 64), np.float32)
    for t in range(bricks):
        for v in range(16):
            picks[0, t * 16 + v, t * 64 + v] = 1
            picks[1, t * 16 + v, t * 64 + (v // 4) * 16 + v % 4] = 1
            picks[2, t * 16 + v, t * 64 + v] = 1
    return picks.reshape(3 * bricks * 16, bricks * 64)


def chunks_of(rows, count):
    units = rows // 16
    cuts = [round(units * q / count) * 16 for q in range(count + 1)]
    return [(lo, hi - lo) for lo, hi in zip(cuts[:-1], cuts[1:])]


def dot(a, b):
    return jnp.dot(a, b, preferred_element_type=F32)


def dot_nt(a, b):
    return lax.dot_general(a, b, (((1,), (1,)), ((), ())), preferred_element_type=F32)


def dot_tn(a, b):
    return lax.dot_general(a, b, (((0,), (0,)), ((), ())), preferred_element_type=F32)


def make_kernel(ngx, ngy, bricks, local_count, remote_count, channels, chunk_count):
    rows = bricks * 64
    frows = bricks * 16
    share = 27 * channels // ngx
    half = 128
    left = -(-share // 16) * 16
    right = -(-share // 32) * 16
    padded = left + right
    wide = 2 * half
    chips = ngx // 2
    outer = ngx // 4
    chunks = chunks_of(padded, chunk_count)
    nq = len(chunks)
    ext = rows + 3 * frows

    def kernel(
        valid, lrules, lcodes, rrules, rcodes,
        feat, weight, cot, blocks, perm, picks, picks_t, slot_of, eye, twice,
        out, fgrad, wgrad,
        w_ref, x_ref, xt_ref, m_ref, g_ref, t_ref, ge, gface, frecv, fsend, totals, fcls,
        wg, buf, recv_a, acc, recv_b, acc2, recv_c, final, summed,
        s_g, r_g, s_f, r_f, s_a, r_a, s_b, r_b, s_c, r_c, s_d, r_d,
    ):
        i = lax.axis_index("gx")
        j = lax.axis_index("gy")
        core = lax.rem(i, 2)
        inner = lax.rem(i // 2, 2)
        z = i // 4
        up_i, dn_i = lax.rem(i + 1, ngx), lax.rem(i + ngx - 1, ngx)
        up_j, dn_j = lax.rem(j + 1, ngy), lax.rem(j + ngy - 1, ngy)
        ups = [(up_i, j), (i, up_j), (up_i, up_j)]
        downs = [(dn_i, j), (i, dn_j), (dn_i, dn_j)]
        core_peer = (i + 1 - 2 * core, j)
        inner_peer = (i + 2 - 4 * inner, j)
        outer_peers = [(lax.rem(i + 4 * k, ngx), j) for k in range(1, outer)]
        gy_peers = [(i, lax.rem(j + k, ngy)) for k in range(1, ngy)]
        peers = ups + downs + [core_peer, inner_peer] + outer_peers + gy_peers

        barrier = pltpu.get_barrier_semaphore()
        for peer in peers:
            pl.semaphore_signal(barrier, inc=1, device_id=peer, device_id_type=MESH)

        live = [valid[0, 0, s] for s in range(bricks)]
        live_f = [v.astype(F32) for v in live]
        for s in range(bricks):
            ge[s * 64 : (s + 1) * 64] = (cot[0, 0, s].astype(F32) * live_f[s]).astype(BF)
        own = ge[0:rows]
        for tap in range(27):
            w_ref[tap] = weight[:, tap * channels : (tap + 1) * channels]
        gface[...] = dot(picks[0 : 2 * frows], own).astype(BF)
        pl.semaphore_wait(barrier, len(peers))

        def remote(src, dst, ssem, rsem, peer):
            return pltpu.make_async_remote_copy(
                src_ref=src, dst_ref=dst, send_sem=ssem, recv_sem=rsem,
                device_id=peer, device_id_type=MESH,
            )

        face_copies = []
        for c in range(3):
            src = gface.at[pl.ds(frows * (c % 2), frows)]
            dst = ge.at[pl.ds(rows + c * frows, frows)]
            copy = remote(src, dst, s_g.at[c], r_g.at[c], downs[c])
            copy.start()
            face_copies.append(copy)

        for s in range(bricks):
            moved = dot_nt(perm[...], feat[0, 0, s]) * live_f[s]
            for cls in range(8):
                x_ref[cls, s * 64 : (s + 1) * 64] = moved[cls * 64 : (cls + 1) * 64].astype(BF)
        for cls in range(8):
            xt_ref[cls] = dot_nt(eye[...], x_ref[cls]).astype(BF)

        groups = 8 * bricks
        row_id = lax.broadcasted_iota(jnp.int32, (4 * groups, 128), 0)
        lane_id = lax.broadcasted_iota(jnp.int32, (4 * groups, 128), 1)
        counts = jnp.zeros((4 * groups, 128), F32)

        def count(total, kind, source, target, code):
            at = jnp.where(target < bricks, kind * groups + 8 * target + code, -1)
            return total + jnp.where((row_id == at) & (lane_id == source), 1.0, 0.0)

        for e in range(local_count):
            counts = count(counts, 0, lrules[0, 0, 0, e], lrules[0, 0, 1, e], lcodes[0, 0, e])
        for c in range(3):
            for e in range(remote_count):
                counts = count(
                    counts, c + 1, rrules[0, 0, c, 0, e], rrules[0, 0, c, 1, e], rcodes[0, c, 0, e]
                )
        spread = dot(counts.astype(BF), slot_of[...])

        for d in range(8):
            codes = [k for k in range(8) if k & ~d == 0]
            full = {k: blocks[PAIR_AT[(d, k)]].astype(F32) for k in codes}
            for kind in range(4):
                need = (0, 1, 2, 3)[kind]
                lo, hi = ((0, 64), (0, 16), (64, 80), (0, 16))[kind]
                for t in range(bricks):
                    total = jnp.zeros((hi - lo, rows), F32)
                    for k in codes:
                        if k & need == need:
                            at = kind * groups + 8 * t + k
                            total = total + spread[at : at + 1] * full[k][lo:hi]
                    first = t * 64 if kind == 0 else rows + (kind - 1) * frows + t * 16
                    m_ref[d, first : first + hi - lo] = total.astype(BF)

        for copy in face_copies:
            copy.wait()
        grads = dot(ge[...], twice[...]).astype(BF)
        for d in range(8):
            g_ref[d] = dot_tn(m_ref[d], grads).astype(BF)

        a_copies = []
        built = 0
        first_lanes = lax.broadcasted_iota(jnp.int32, (right, half), 1) < channels - half
        for tap, cls, shift in TAPS:
            wg[tap * channels : (tap + 1) * channels] = dot(xt_ref[cls], g_ref[shift])
            while built < chips and 2 * share * (built + 1) <= (tap + 1) * channels:
                for h in range(2):
                    first = share * (2 * built + h)
                    block = wg[first : first + share, 0:half].astype(BF)
                    tail = wg[first : first + share, half:wide]
                    fill = jnp.zeros((left - share, half), BF)
                    buf[2 * built + h, 0:left] = jnp.concatenate([block, fill], axis=0)
                    rest = jnp.zeros((2 * right - share, half), F32)
                    later = jnp.concatenate([tail[right:share], rest], axis=0)
                    packed = jnp.where(first_lanes, tail[0:right], later)
                    buf[2 * built + h, left:padded] = packed.astype(BF)
                copy = remote(
                    buf.at[2 * built + 1 - core], recv_a.at[built],
                    s_a.at[built], r_a.at[built], core_peer,
                )
                copy.start()
                a_copies.append(copy)
                built += 1

        for d in range(8):
            total = None
            for tap, cls, shift in TAPS:
                if shift == d:
                    term = dot_nt(x_ref[cls], w_ref[tap])
                    total = term if total is None else total + term
            t_ref[d] = total

        for copy in a_copies:
            copy.wait_recv()
        b_copies = []
        for q, (lo, n) in enumerate(chunks):
            for m in range(chips):
                mine = buf[2 * m + core, lo : lo + n].astype(F32)
                acc[m % 2, m // 2, lo : lo + n] = (
                    mine + recv_a[m, lo : lo + n].astype(F32)
                ).astype(BF)
            copy = remote(
                acc.at[1 - inner, :, pl.ds(lo, n)], recv_b.at[:, pl.ds(lo, n)],
                s_b.at[q], r_b.at[q], inner_peer,
            )
            copy.start()
            b_copies.append(copy)

        total = None
        for d in range(8):
            value = t_ref[d]
            high = value.astype(BF)
            low = (value - high.astype(F32)).astype(BF)
            term = dot(m_ref[d], high) + dot(m_ref[d], low)
            total = term if total is None else total + term
        totals[...] = total[0:rows]
        fsend[...] = total[rows:ext].astype(BF)
        f_copies = []
        for c in range(3):
            span = pl.ds(c * frows, frows)
            copy = remote(fsend.at[span], frecv.at[span], s_f.at[c], r_f.at[c], ups[c])
            copy.start()
            f_copies.append(copy)

        def second(q):
            lo, n = chunks[q]
            b_copies[q].wait_recv()
            for o in range(outer):
                acc2[o, lo : lo + n] = (
                    acc[inner, o, lo : lo + n].astype(F32) + recv_b[o, lo : lo + n].astype(F32)
                ).astype(BF)
            started = []
            for k in range(1, outer):
                copy = remote(
                    acc2.at[lax.rem(z + k, outer), pl.ds(lo, n)], recv_c.at[k - 1, pl.ds(lo, n)],
                    s_c.at[q, k - 1], r_c.at[q, k - 1], outer_peers[k - 1],
                )
                copy.start()
                started.append(copy)
            return started

        def third(q):
            lo, n = chunks[q]
            total = acc2[z, lo : lo + n].astype(F32)
            for k in range(1, outer):
                c_copies[q][k - 1].wait_recv()
                total = total + recv_c[k - 1, lo : lo + n].astype(F32)
            final[j, lo : lo + n] = total.astype(BF)
            started = []
            for k in range(1, ngy):
                mine = final.at[j, pl.ds(lo, n)]
                copy = remote(mine, mine, s_d.at[q, k - 1], r_d.at[q, k - 1], gy_peers[k - 1])
                copy.start()
                started.append(copy)
            return started

        def feature_class(cls):
            total = None
            for tap, tap_cls, shift in TAPS:
                if tap_cls == cls:
                    term = dot(g_ref[shift, :, 0:channels], w_ref[tap])
                    total = term if total is None else total + term
            for s in range(bricks):
                fcls[s, cls * 64 : (cls + 1) * 64] = (
                    total[s * 64 : (s + 1) * 64] * live_f[s]
                ).astype(BF)

        c_copies = []
        for cls in range(4):
            feature_class(cls)
        c_copies.append(second(0))
        for cls in range(4, 7):
            feature_class(cls)
        for q in range(1, nq):
            c_copies.append(second(q))
            if q == 1:
                feature_class(7)
        for s in range(bricks):
            fgrad[0, 0, s] = dot_tn(fcls[s], perm[...]).astype(BF)

        for copy in f_copies:
            copy.wait()
        result = totals[...] + dot(picks_t[...], frecv[...])
        for s in range(bricks):
            out[0, 0, s] = (result[s * 64 : (s + 1) * 64] * live_f[s]).astype(BF)

        d_copies = [third(q) for q in range(nq)]
        for q, (lo, n) in enumerate(chunks):
            for copy in d_copies[q]:
                copy.wait_recv()
            total = final[0, lo : lo + n].astype(F32)
            for k in range(1, ngy):
                total = total + final[k, lo : lo + n].astype(F32)
            summed[lo : lo + n] = total
        wgrad[0:half] = jnp.transpose(summed[0:left])[:, 0:share]
        turned = jnp.transpose(summed[left:padded])
        tail = channels - half
        wgrad[half:channels, 0:right] = turned[0:tail]
        wgrad[half:channels, right:share] = turned[tail : 2 * tail, 0 : share - right]

        for copy in a_copies + b_copies:
            copy.wait_send()
        for copies in c_copies + d_copies:
            for copy in copies:
                copy.wait_send()

    dma = pltpu.SemaphoreType.DMA
    scratch = [
        pltpu.VMEM((27, channels, channels), BF),
        pltpu.VMEM((8, rows, channels), BF),
        pltpu.VMEM((8, channels, rows), BF),
        pltpu.VMEM((8, ext, rows), BF),
        pltpu.VMEM((8, rows, wide), BF),
        pltpu.VMEM((8, rows, channels), F32),
        pltpu.VMEM((ext, channels), BF),
        pltpu.VMEM((2 * frows, channels), BF),
        pltpu.VMEM((3 * frows, channels), BF),
        pltpu.VMEM((3 * frows, channels), BF),
        pltpu.VMEM((rows, channels), F32),
        pltpu.VMEM((bricks, 512, channels), BF),
        pltpu.VMEM((27 * channels, wide), F32),
        pltpu.VMEM((ngx, padded, half), BF),
        pltpu.VMEM((chips, padded, half), BF),
        pltpu.VMEM((2, outer, padded, half), BF),
        pltpu.VMEM((outer, padded, half), BF),
        pltpu.VMEM((outer, padded, half), BF),
        pltpu.VMEM((outer - 1, padded, half), BF),
        pltpu.VMEM((ngy, padded, half), BF),
        pltpu.VMEM((padded, half), F32),
        dma((3,)), dma((3,)), dma((3,)), dma((3,)),
        dma((chips,)), dma((chips,)), dma((nq,)), dma((nq,)),
        dma((nq, outer - 1)), dma((nq, outer - 1)),
        dma((nq, ngy - 1)), dma((nq, ngy - 1)),
    ]
    return kernel, scratch, share


def solution(mesh):
    ngx, ngy = mesh.shape["gx"], mesh.shape["gy"]

    def shards(
        features, weight, cotangent, valid, local_rules, local_codes, remote_rules, remote_codes
    ):
        bricks = features.shape[2]
        channels = features.shape[-1]
        local_count = local_codes.shape[-1]
        remote_count = remote_codes.shape[-1]
        kernel, scratch, share = make_kernel(
            ngx, ngy, bricks, local_count, remote_count, channels, 4
        )
        order = parity_order()
        perm = np.zeros((512, 512), np.float32)
        perm[np.arange(512), order] = 1
        picks = face_picks(bricks)
        slot_of = (np.arange(128)[:, None] == (np.arange(bricks * 64) // 64)[None, :]).astype(
            np.float32
        )
        twice = np.zeros((channels, 256), np.float32)
        twice[np.arange(channels), np.arange(channels)] = 1
        twice[np.arange(128, channels), np.arange(128, channels) + channels - 128] = 1
        consts = [
            jnp.asarray(c, BF)
            for c in (
                rule_blocks(bricks), perm, picks, picks.T, slot_of,
                np.eye(channels, dtype=np.float32), twice,
            )
        ]
        vmem = pl.BlockSpec(memory_space=pltpu.VMEM)
        smem = pl.BlockSpec(memory_space=pltpu.SMEM)
        out, fgrad, wgrad = pl.pallas_call(
            kernel,
            out_shape=(
                jax.ShapeDtypeStruct(cotangent.shape, BF),
                jax.ShapeDtypeStruct((1, 1, bricks, channels, 512), BF),
                jax.ShapeDtypeStruct((channels, share), F32),
            ),
            in_specs=[smem] * 5 + [vmem] * 10,
            out_specs=(vmem, vmem, vmem),
            scratch_shapes=scratch,
            compiler_params=pltpu.CompilerParams(
                collective_id=0, has_side_effects=True, vmem_limit_bytes=56 * 1024 * 1024
            ),
        )(
            valid, local_rules, local_codes, jnp.swapaxes(remote_rules, 2, 3),
            jnp.swapaxes(remote_codes, 1, 2), jnp.swapaxes(features, 3, 4), weight.T,
            cotangent, *consts,
        )
        return out, jnp.swapaxes(fgrad, 3, 4), wgrad.T

    return jax.shard_map(
        shards,
        mesh=mesh,
        in_specs=(
            P("gx", "gy", None, None, None),
            P(),
            P("gx", "gy", None, None, None),
            P("gx", "gy", None),
            P("gx", "gy", None, None),
            P("gx", "gy", None),
            P("gx", "gy", None, None, None),
            P("gx", "gy", None, None),
        ),
        out_specs=(P("gx", "gy", None, None, None), P("gx", "gy", None, None, None), P("gx", None)),
        check_vma=False,
    )
```

```python
import jax
import jax.numpy as jnp
import numpy as np
from jax import lax
from jax.experimental import pallas as pl
from jax.experimental.pallas import tpu as pltpu
from jax.sharding import PartitionSpec as P

BF = jnp.bfloat16
F32 = jnp.float32
MESH = pl.DeviceIdType.MESH

PAIRS = [(d, k) for d in range(8) for k in range(8) if k & ~d == 0]
PAIR_AT = {pair: at for at, pair in enumerate(PAIRS)}


def tap_list():
    taps = []
    for e in range(3):
        for f in range(3):
            for g in range(3):
                cls = (e != 1) + 2 * (f != 1) + 4 * (g != 1)
                shift = (e == 0) + 2 * (f == 0) + 4 * (g == 0)
                taps.append((9 * e + 3 * f + g, int(cls), int(shift)))
    return taps


TAPS = tap_list()


def bits(k):
    return k % 2, k // 2 % 2, k // 4


def rule_blocks(bricks):
    v = np.arange(64)
    coords = [v // 16, v // 4 % 4, v % 4]
    face = np.concatenate([v, (np.arange(16) // 4) * 16 + np.arange(16) % 4])
    blocks = []
    for d, k in PAIRS:
        hit = np.ones((64, 64), bool)
        for axis in range(3):
            row = coords[axis][:, None] + 4 * bits(k)[axis]
            col = coords[axis][None, :] + bits(d)[axis]
            hit &= row == col
        blocks.append(np.tile(hit[face], (1, bricks)))
    return np.stack(blocks).astype(np.float32)


def parity_order():
    rows = np.zeros(512, np.int64)
    for cls in range(8):
        px, py, pz = bits(cls)
        for v in range(64):
            a, b, c = v // 16, v // 4 % 4, v % 4
            rows[cls * 64 + v] = (2 * a + px) * 64 + (2 * b + py) * 8 + 2 * c + pz
    return rows


def face_picks(bricks):
    picks = np.zeros((3, bricks * 16, bricks * 64), np.float32)
    for t in range(bricks):
        for v in range(16):
            picks[0, t * 16 + v, t * 64 + v] = 1
            picks[1, t * 16 + v, t * 64 + (v // 4) * 16 + v % 4] = 1
            picks[2, t * 16 + v, t * 64 + v] = 1
    return picks.reshape(3 * bricks * 16, bricks * 64)


def chunks_of(rows, count):
    units = rows // 16
    cuts = [round(units * q / count) * 16 for q in range(count + 1)]
    return [(lo, hi - lo) for lo, hi in zip(cuts[:-1], cuts[1:])]


def dot(a, b):
    return jnp.dot(a, b, preferred_element_type=F32)


def dot_nt(a, b):
    return lax.dot_general(a, b, (((1,), (1,)), ((), ())), preferred_element_type=F32)


def dot_tn(a, b):
    return lax.dot_general(a, b, (((0,), (0,)), ((), ())), preferred_element_type=F32)


def make_kernel(ngx, ngy, bricks, local_count, remote_count, channels, chunk_count):
    rows = bricks * 64
    frows = bricks * 16
    share = 27 * channels // ngx
    half = 128
    left = -(-share // 16) * 16
    right = -(-share // 32) * 16
    padded = left + right
    wide = 2 * half
    chips = ngx // 2
    outer = ngx // 4
    part = 16 * max(1, padded // (32 * ngy))
    base = padded - part * ngy
    chunks = chunks_of(base, min(chunk_count, base // 16))
    nq = len(chunks)
    parts = chunks_of(part, min(chunk_count, part // 16))
    np_ = len(parts)
    ext = rows + 3 * frows

    def kernel(
        valid, lrules, lcodes, rrules, rcodes,
        feat, weight_hbm, cot, blocks, perm, picks, picks_t, slot_of, eye, twice,
        out, fgrad, wgrad,
        weight, w_ref, x_ref, xt_ref, m_ref, g_ref, t_ref, ge, gface, frecv, fsend, totals, fcls,
        wg, buf, recv_a, acc, recv_b, acc2, recv_c, final, summed,
        xacc, recv_x, yacc, recv_y, zacc, recv_z, gathered,
        s_g, r_g, s_f, r_f, s_a, r_a, s_b, r_b, s_c, r_c, s_d, r_d,
        s_x, r_x, s_y, r_y, s_z, r_z, s_w, r_w, s_fetch,
    ):
        i = lax.axis_index("gx")
        j = lax.axis_index("gy")
        core = lax.rem(i, 2)
        inner = lax.rem(i // 2, 2)
        z = i // 4
        up_i, dn_i = lax.rem(i + 1, ngx), lax.rem(i + ngx - 1, ngx)
        up_j, dn_j = lax.rem(j + 1, ngy), lax.rem(j + ngy - 1, ngy)
        ups = [(up_i, j), (i, up_j), (up_i, up_j)]
        downs = [(dn_i, j), (i, dn_j), (dn_i, dn_j)]
        core_peer = (i + 1 - 2 * core, j)
        inner_peer = (i + 2 - 4 * inner, j)
        outer_peers = [(lax.rem(i + 4 * k, ngx), j) for k in range(1, outer)]
        gy_peers = [(i, lax.rem(j + k, ngy)) for k in range(1, ngy)]
        peers = ups + downs + [core_peer, inner_peer] + outer_peers + gy_peers

        fetch = pltpu.make_async_copy(weight_hbm, weight, s_fetch)
        fetch.start()
        barrier = pltpu.get_barrier_semaphore()
        for peer in peers:
            pl.semaphore_signal(barrier, inc=1, device_id=peer, device_id_type=MESH)

        live = [valid[0, 0, s] for s in range(bricks)]
        live_f = [v.astype(F32) for v in live]
        for s in range(bricks):
            ge[s * 64 : (s + 1) * 64] = (cot[0, 0, s].astype(F32) * live_f[s]).astype(BF)
        own = ge[0:rows]
        gface[...] = dot(picks[0 : 2 * frows], own).astype(BF)
        pl.semaphore_wait(barrier, len(peers))

        def remote(src, dst, ssem, rsem, peer):
            return pltpu.make_async_remote_copy(
                src_ref=src, dst_ref=dst, send_sem=ssem, recv_sem=rsem,
                device_id=peer, device_id_type=MESH,
            )

        face_copies = []
        for c in range(3):
            src = gface.at[pl.ds(frows * (c % 2), frows)]
            dst = ge.at[pl.ds(rows + c * frows, frows)]
            copy = remote(src, dst, s_g.at[c], r_g.at[c], downs[c])
            copy.start()
            face_copies.append(copy)

        for s in range(bricks):
            moved = dot_nt(perm[...], feat[0, 0, s]) * live_f[s]
            for cls in range(8):
                x_ref[cls, s * 64 : (s + 1) * 64] = moved[cls * 64 : (cls + 1) * 64].astype(BF)
        for cls in range(8):
            xt_ref[cls] = dot_nt(eye[...], x_ref[cls]).astype(BF)

        groups = 8 * bricks
        row_id = lax.broadcasted_iota(jnp.int32, (4 * groups, 128), 0)
        lane_id = lax.broadcasted_iota(jnp.int32, (4 * groups, 128), 1)
        counts = jnp.zeros((4 * groups, 128), F32)

        def count(total, kind, source, target, code):
            at = jnp.where(target < bricks, kind * groups + 8 * target + code, -1)
            return total + jnp.where((row_id == at) & (lane_id == source), 1.0, 0.0)

        for e in range(local_count):
            counts = count(counts, 0, lrules[0, 0, 0, e], lrules[0, 0, 1, e], lcodes[0, 0, e])
        for c in range(3):
            for e in range(remote_count):
                counts = count(
                    counts, c + 1, rrules[0, 0, c, 0, e], rrules[0, 0, c, 1, e], rcodes[0, c, 0, e]
                )
        spread = dot(counts.astype(BF), slot_of[...])

        for d in range(8):
            codes = [k for k in range(8) if k & ~d == 0]
            full = {k: blocks[PAIR_AT[(d, k)]].astype(F32) for k in codes}
            for kind in range(4):
                need = (0, 1, 2, 3)[kind]
                lo, hi = ((0, 64), (0, 16), (64, 80), (0, 16))[kind]
                for t in range(bricks):
                    total = jnp.zeros((hi - lo, rows), F32)
                    for k in codes:
                        if k & need == need:
                            at = kind * groups + 8 * t + k
                            total = total + spread[at : at + 1] * full[k][lo:hi]
                    first = t * 64 if kind == 0 else rows + (kind - 1) * frows + t * 16
                    m_ref[d, first : first + hi - lo] = total.astype(BF)

        for copy in face_copies:
            copy.wait()
        grads = dot(ge[...], twice[...]).astype(BF)
        for d in range(8):
            g_ref[d] = dot_tn(m_ref[d], grads).astype(BF)

        a_copies = []
        built = 0
        first_lanes = lax.broadcasted_iota(jnp.int32, (right, half), 1) < channels - half
        for tap, cls, shift in TAPS:
            wg[tap * channels : (tap + 1) * channels] = dot(xt_ref[cls], g_ref[shift])
            while built < chips and 2 * share * (built + 1) <= (tap + 1) * channels:
                for h in range(2):
                    first = share * (2 * built + h)
                    block = wg[first : first + share, 0:half].astype(BF)
                    tail = wg[first : first + share, half:wide]
                    fill = jnp.zeros((left - share, half), BF)
                    buf[2 * built + h, 0:left] = jnp.concatenate([block, fill], axis=0)
                    rest = jnp.zeros((2 * right - share, half), F32)
                    later = jnp.concatenate([tail[right:share], rest], axis=0)
                    packed = jnp.where(first_lanes, tail[0:right], later)
                    buf[2 * built + h, left:padded] = packed.astype(BF)
                copy = remote(
                    buf.at[2 * built + 1 - core], recv_a.at[built],
                    s_a.at[built], r_a.at[built], core_peer,
                )
                copy.start()
                a_copies.append(copy)
                built += 1

        fetch.wait()
        for tap in range(27):
            w_ref[tap] = weight[:, tap * channels : (tap + 1) * channels]

        def forward(d):
            total = None
            for tap, cls, shift in TAPS:
                if shift == d:
                    term = dot_nt(x_ref[cls], w_ref[tap])
                    total = term if total is None else total + term
            t_ref[d] = total

        for copy in a_copies:
            copy.wait_recv()

        def core_sum(m, lo, n):
            mine = buf[2 * m + core, lo : lo + n].astype(F32)
            return (mine + recv_a[m, lo : lo + n].astype(F32)).astype(BF)

        x_copies, b_copies = [], []
        for q in range(max(nq, np_)):
            if q < np_:
                lo, n = parts[q]
                for m in range(chips):
                    for g in range(ngy):
                        xacc[g, m % 2, m // 2, lo : lo + n] = core_sum(m, base + g * part + lo, n)
                started = []
                for k in range(1, ngy):
                    copy = remote(
                        xacc.at[lax.rem(j + k, ngy), :, :, pl.ds(lo, n)],
                        recv_x.at[k - 1, :, :, pl.ds(lo, n)],
                        s_x.at[q, k - 1], r_x.at[q, k - 1], gy_peers[k - 1],
                    )
                    copy.start()
                    started.append(copy)
                x_copies.append(started)
            if q < nq:
                lo, n = chunks[q]
                for m in range(chips):
                    acc[m % 2, m // 2, lo : lo + n] = core_sum(m, lo, n)
                copy = remote(
                    acc.at[1 - inner, :, pl.ds(lo, n)], recv_b.at[:, pl.ds(lo, n)],
                    s_b.at[q], r_b.at[q], inner_peer,
                )
                copy.start()
                b_copies.append(copy)

        for d in range(8):
            forward(d)

        total = None
        for d in range(8):
            value = t_ref[d]
            high = value.astype(BF)
            low = (value - high.astype(F32)).astype(BF)
            term = dot(m_ref[d], high) + dot(m_ref[d], low)
            total = term if total is None else total + term
        totals[...] = total[0:rows]
        fsend[...] = total[rows:ext].astype(BF)
        f_copies = []
        for c in range(3):
            span = pl.ds(c * frows, frows)
            copy = remote(fsend.at[span], frecv.at[span], s_f.at[c], r_f.at[c], ups[c])
            copy.start()
            f_copies.append(copy)

        def second(q):
            lo, n = chunks[q]
            b_copies[q].wait_recv()
            for o in range(outer):
                acc2[o, lo : lo + n] = (
                    acc[inner, o, lo : lo + n].astype(F32) + recv_b[o, lo : lo + n].astype(F32)
                ).astype(BF)
            started = []
            for k in range(1, outer):
                copy = remote(
                    acc2.at[lax.rem(z + k, outer), pl.ds(lo, n)], recv_c.at[k - 1, pl.ds(lo, n)],
                    s_c.at[q, k - 1], r_c.at[q, k - 1], outer_peers[k - 1],
                )
                copy.start()
                started.append(copy)
            return started

        def third(q):
            lo, n = chunks[q]
            total = acc2[z, lo : lo + n].astype(F32)
            for k in range(1, outer):
                c_copies[q][k - 1].wait_recv()
                total = total + recv_c[k - 1, lo : lo + n].astype(F32)
            final[j, lo : lo + n] = total.astype(BF)
            started = []
            for k in range(1, ngy):
                mine = final.at[j, pl.ds(lo, n)]
                copy = remote(mine, mine, s_d.at[q, k - 1], r_d.at[q, k - 1], gy_peers[k - 1])
                copy.start()
                started.append(copy)
            return started

        def part_x(q):
            lo, n = parts[q]
            for copy in x_copies[q]:
                copy.wait_recv()
            for h in range(2):
                for o in range(outer):
                    total = xacc[j, h, o, lo : lo + n].astype(F32)
                    for k in range(1, ngy):
                        total = total + recv_x[k - 1, h, o, lo : lo + n].astype(F32)
                    yacc[h, o, lo : lo + n] = total.astype(BF)
            copy = remote(
                yacc.at[1 - inner, :, pl.ds(lo, n)], recv_y.at[:, pl.ds(lo, n)],
                s_y.at[q], r_y.at[q], inner_peer,
            )
            copy.start()
            return copy

        def part_y(q):
            lo, n = parts[q]
            y_copies[q].wait_recv()
            for o in range(outer):
                zacc[o, lo : lo + n] = (
                    yacc[inner, o, lo : lo + n].astype(F32) + recv_y[o, lo : lo + n].astype(F32)
                ).astype(BF)
            started = []
            for k in range(1, outer):
                copy = remote(
                    zacc.at[lax.rem(z + k, outer), pl.ds(lo, n)], recv_z.at[k - 1, pl.ds(lo, n)],
                    s_z.at[q, k - 1], r_z.at[q, k - 1], outer_peers[k - 1],
                )
                copy.start()
                started.append(copy)
            return started

        def part_z(q):
            lo, n = parts[q]
            total = zacc[z, lo : lo + n].astype(F32)
            for k in range(1, outer):
                z_copies[q][k - 1].wait_recv()
                total = total + recv_z[k - 1, lo : lo + n].astype(F32)
            gathered[j, lo : lo + n] = total
            started = []
            for k in range(1, ngy):
                mine = gathered.at[j, pl.ds(lo, n)]
                copy = remote(mine, mine, s_w.at[q, k - 1], r_w.at[q, k - 1], gy_peers[k - 1])
                copy.start()
                started.append(copy)
            return started

        def feature_class(cls):
            total = None
            for tap, tap_cls, shift in TAPS:
                if tap_cls == cls:
                    term = dot(g_ref[shift, :, 0:channels], w_ref[tap])
                    total = term if total is None else total + term
            for s in range(bricks):
                fcls[s, cls * 64 : (cls + 1) * 64] = (
                    total[s * 64 : (s + 1) * 64] * live_f[s]
                ).astype(BF)

        c_copies, d_copies, y_copies, z_copies, w_copies = [], [], [], [], []
        feature_class(0)
        feature_class(1)
        for q in range(max(nq, np_)):
            if q < nq:
                c_copies.append(second(q))
            if q < np_:
                y_copies.append(part_x(q))
            for cls in (2, 3, 4) if q == 0 else (5, 6) if q == 1 else ():
                feature_class(cls)
        for cls in range(5, 8) if max(nq, np_) == 1 else (7,):
            feature_class(cls)
        for q in range(max(nq, np_)):
            if q < np_:
                z_copies.append(part_y(q))
            if q == 0:
                for s in range(bricks):
                    fgrad[0, 0, s] = dot_tn(fcls[s], perm[...]).astype(BF)
            if q < nq:
                d_copies.append(third(q))
        for copy in f_copies:
            copy.wait()
        result = totals[...] + dot(picks_t[...], frecv[...])
        for s in range(bricks):
            out[0, 0, s] = (result[s * 64 : (s + 1) * 64] * live_f[s]).astype(BF)
        for q in range(np_):
            w_copies.append(part_z(q))

        for q, (lo, n) in enumerate(chunks):
            for copy in d_copies[q]:
                copy.wait_recv()
            total = final[0, lo : lo + n].astype(F32)
            for k in range(1, ngy):
                total = total + final[k, lo : lo + n].astype(F32)
            summed[lo : lo + n] = total
        for copies in w_copies:
            for copy in copies:
                copy.wait_recv()
        for g in range(ngy):
            summed[base + g * part : base + (g + 1) * part] = gathered[g]
        wgrad[0:half] = jnp.transpose(summed[0:left])[:, 0:share]
        turned = jnp.transpose(summed[left:padded])
        tail = channels - half
        wgrad[half:channels, 0:right] = turned[0:tail]
        wgrad[half:channels, right:share] = turned[tail : 2 * tail, 0 : share - right]

        for copy in a_copies + b_copies + y_copies:
            copy.wait_send()
        for copies in c_copies + d_copies + x_copies + z_copies + w_copies:
            for copy in copies:
                copy.wait_send()

    dma = pltpu.SemaphoreType.DMA
    scratch = [
        pltpu.VMEM((channels, 27 * channels), BF),
        pltpu.VMEM((27, channels, channels), BF),
        pltpu.VMEM((8, rows, channels), BF),
        pltpu.VMEM((8, channels, rows), BF),
        pltpu.VMEM((8, ext, rows), BF),
        pltpu.VMEM((8, rows, wide), BF),
        pltpu.VMEM((8, rows, channels), F32),
        pltpu.VMEM((ext, channels), BF),
        pltpu.VMEM((2 * frows, channels), BF),
        pltpu.VMEM((3 * frows, channels), BF),
        pltpu.VMEM((3 * frows, channels), BF),
        pltpu.VMEM((rows, channels), F32),
        pltpu.VMEM((bricks, 512, channels), BF),
        pltpu.VMEM((27 * channels, wide), F32),
        pltpu.VMEM((ngx, padded, half), BF),
        pltpu.VMEM((chips, padded, half), BF),
        pltpu.VMEM((2, outer, base, half), BF),
        pltpu.VMEM((outer, base, half), BF),
        pltpu.VMEM((outer, base, half), BF),
        pltpu.VMEM((outer - 1, base, half), BF),
        pltpu.VMEM((ngy, base, half), BF),
        pltpu.VMEM((padded, half), F32),
        pltpu.VMEM((ngy, 2, outer, part, half), BF),
        pltpu.VMEM((ngy - 1, 2, outer, part, half), BF),
        pltpu.VMEM((2, outer, part, half), BF),
        pltpu.VMEM((outer, part, half), BF),
        pltpu.VMEM((outer, part, half), BF),
        pltpu.VMEM((outer - 1, part, half), BF),
        pltpu.VMEM((ngy, part, half), F32),
        dma((3,)), dma((3,)), dma((3,)), dma((3,)),
        dma((chips,)), dma((chips,)), dma((nq,)), dma((nq,)),
        dma((nq, outer - 1)), dma((nq, outer - 1)),
        dma((nq, ngy - 1)), dma((nq, ngy - 1)),
        dma((np_, ngy - 1)), dma((np_, ngy - 1)), dma((np_,)), dma((np_,)),
        dma((np_, outer - 1)), dma((np_, outer - 1)), dma((np_, ngy - 1)), dma((np_, ngy - 1)),
        dma,
    ]
    return kernel, scratch, share


def hand_over(a, b, c, a_out, b_out, c_out, sems):
    pairs = ((a, a_out), (b, b_out), (c, c_out))
    copies = [pltpu.make_async_copy(src, dst, sems.at[at]) for at, (src, dst) in enumerate(pairs)]
    for copy in copies:
        copy.start()
    for copy in copies:
        copy.wait()


def solution(mesh):
    ngx, ngy = mesh.shape["gx"], mesh.shape["gy"]

    def shards(
        features, weight, cotangent, valid, local_rules, local_codes, remote_rules, remote_codes
    ):
        bricks = features.shape[2]
        channels = features.shape[-1]
        local_count = local_codes.shape[-1]
        remote_count = remote_codes.shape[-1]
        kernel, scratch, share = make_kernel(
            ngx, ngy, bricks, local_count, remote_count, channels, 2
        )
        order = parity_order()
        perm = np.zeros((512, 512), np.float32)
        perm[np.arange(512), order] = 1
        picks = face_picks(bricks)
        slot_of = (np.arange(128)[:, None] == (np.arange(bricks * 64) // 64)[None, :]).astype(
            np.float32
        )
        twice = np.zeros((channels, 256), np.float32)
        twice[np.arange(channels), np.arange(channels)] = 1
        twice[np.arange(128, channels), np.arange(128, channels) + channels - 128] = 1
        consts = [
            jnp.asarray(c, BF)
            for c in (
                rule_blocks(bricks), perm, picks, picks.T, slot_of,
                np.eye(channels, dtype=np.float32), twice,
            )
        ]
        vmem = pl.BlockSpec(memory_space=pltpu.VMEM)
        anywhere = pl.BlockSpec(memory_space=pl.ANY)
        hbm = pl.BlockSpec(memory_space=pltpu.HBM)
        smem = pl.BlockSpec(memory_space=pltpu.SMEM)
        out, fgrad, wgrad = pl.pallas_call(
            kernel,
            out_shape=(
                jax.ShapeDtypeStruct(cotangent.shape, BF),
                jax.ShapeDtypeStruct((1, 1, bricks, channels, 512), BF),
                jax.ShapeDtypeStruct((channels, share), F32),
            ),
            in_specs=[smem] * 5 + [vmem, anywhere] + [vmem] * 8,
            out_specs=(vmem, vmem, vmem),
            scratch_shapes=scratch,
            compiler_params=pltpu.CompilerParams(
                collective_id=0, has_side_effects=True, vmem_limit_bytes=56 * 1024 * 1024
            ),
        )(
            valid, local_rules, local_codes, jnp.swapaxes(remote_rules, 2, 3),
            jnp.swapaxes(remote_codes, 1, 2), jnp.swapaxes(features, 3, 4), weight.T,
            cotangent, *consts,
        )
        out, fgrad, wgrad = pl.pallas_call(
            hand_over,
            out_shape=tuple(jax.ShapeDtypeStruct(a.shape, a.dtype) for a in (out, fgrad, wgrad)),
            in_specs=[hbm] * 3,
            out_specs=(hbm,) * 3,
            scratch_shapes=[pltpu.SemaphoreType.DMA((3,))],
        )(out, fgrad, wgrad)
        return out, jnp.swapaxes(fgrad, 3, 4), wgrad.T

    return jax.shard_map(
        shards,
        mesh=mesh,
        in_specs=(
            P("gx", "gy", None, None, None),
            P(),
            P("gx", "gy", None, None, None),
            P("gx", "gy", None),
            P("gx", "gy", None, None),
            P("gx", "gy", None),
            P("gx", "gy", None, None, None),
            P("gx", "gy", None, None),
        ),
        out_specs=(P("gx", "gy", None, None, None), P("gx", "gy", None, None, None), P("gx", None)),
        check_vma=False,
    )
```

```python
import jax
import jax.numpy as jnp
import numpy as np
from jax import lax
from jax.experimental import pallas as pl
from jax.experimental.pallas import tpu as pltpu
from jax.sharding import PartitionSpec as P

BF = jnp.bfloat16
F32 = jnp.float32
MESH = pl.DeviceIdType.MESH

PAIRS = [(d, k) for d in range(8) for k in range(8) if k & ~d == 0]
PAIR_AT = {pair: at for at, pair in enumerate(PAIRS)}


def tap_list():
    taps = []
    for e in range(3):
        for f in range(3):
            for g in range(3):
                cls = (e != 1) + 2 * (f != 1) + 4 * (g != 1)
                shift = (e == 0) + 2 * (f == 0) + 4 * (g == 0)
                taps.append((9 * e + 3 * f + g, int(cls), int(shift)))
    return taps


TAPS = tap_list()


def bits(k):
    return k % 2, k // 2 % 2, k // 4


def rule_blocks(bricks):
    v = np.arange(64)
    coords = [v // 16, v // 4 % 4, v % 4]
    face = np.concatenate([v, (np.arange(16) // 4) * 16 + np.arange(16) % 4])
    blocks = []
    for d, k in PAIRS:
        hit = np.ones((64, 64), bool)
        for axis in range(3):
            row = coords[axis][:, None] + 4 * bits(k)[axis]
            col = coords[axis][None, :] + bits(d)[axis]
            hit &= row == col
        blocks.append(np.tile(hit[face], (1, bricks)))
    return np.stack(blocks).astype(np.float32)


def parity_order():
    rows = np.zeros(512, np.int64)
    for cls in range(8):
        px, py, pz = bits(cls)
        for v in range(64):
            a, b, c = v // 16, v // 4 % 4, v % 4
            rows[cls * 64 + v] = (2 * a + px) * 64 + (2 * b + py) * 8 + 2 * c + pz
    return rows


def face_picks(bricks):
    picks = np.zeros((3, bricks * 16, bricks * 64), np.float32)
    for t in range(bricks):
        for v in range(16):
            picks[0, t * 16 + v, t * 64 + v] = 1
            picks[1, t * 16 + v, t * 64 + (v // 4) * 16 + v % 4] = 1
            picks[2, t * 16 + v, t * 64 + v] = 1
    return picks.reshape(3 * bricks * 16, bricks * 64)


def chunks_of(rows, count):
    units = rows // 16
    cuts = [round(units * q / count) * 16 for q in range(count + 1)]
    return [(lo, hi - lo) for lo, hi in zip(cuts[:-1], cuts[1:])]


def dot(a, b):
    return jnp.dot(a, b, preferred_element_type=F32)


def dot_nt(a, b):
    return lax.dot_general(a, b, (((1,), (1,)), ((), ())), preferred_element_type=F32)


def dot_tn(a, b):
    return lax.dot_general(a, b, (((0,), (0,)), ((), ())), preferred_element_type=F32)


def make_kernel(ngx, ngy, bricks, local_count, remote_count, channels, chunk_count):
    rows = bricks * 64
    frows = bricks * 16
    share = 27 * channels // ngx
    half = 128
    left = -(-share // 16) * 16
    right = -(-share // 32) * 16
    padded = left + right
    wide = 2 * half
    chips = ngx // 2
    outer = ngx // 4
    part = 16 * max(1, padded // (32 * ngy))
    base = padded - part * ngy
    chunks = chunks_of(base, min(chunk_count, base // 16))
    nq = len(chunks)
    parts = chunks_of(part, min(chunk_count, part // 16))
    np_ = len(parts)
    ext = rows + 3 * frows

    def kernel(
        valid, lrules, lcodes, rrules, rcodes,
        feat, weight_hbm, cot, blocks, perm, picks, picks_t, slot_of, eye, twice,
        out, fgrad, wgrad,
        weight, w_ref, x_ref, xt_ref, m_ref, g_ref, t_ref, ge, gface, frecv, fsend, totals, fcls,
        wg, buf, recv_a, acc, recv_b, acc2, recv_c, final, summed,
        xacc, recv_x, yacc, recv_y, zacc, recv_z, gathered,
        s_g, r_g, s_f, r_f, s_a, r_a, s_b, r_b, s_c, r_c, s_d, r_d,
        s_x, r_x, s_y, r_y, s_z, r_z, s_w, r_w, s_fetch,
    ):
        i = lax.axis_index("gx")
        j = lax.axis_index("gy")
        core = lax.rem(i, 2)
        inner = lax.rem(i // 2, 2)
        z = i // 4
        up_i, dn_i = lax.rem(i + 1, ngx), lax.rem(i + ngx - 1, ngx)
        up_j, dn_j = lax.rem(j + 1, ngy), lax.rem(j + ngy - 1, ngy)
        ups = [(up_i, j), (i, up_j), (up_i, up_j)]
        downs = [(dn_i, j), (i, dn_j), (dn_i, dn_j)]
        core_peer = (i + 1 - 2 * core, j)
        inner_peer = (i + 2 - 4 * inner, j)
        outer_peers = [(lax.rem(i + 4 * k, ngx), j) for k in range(1, outer)]
        gy_peers = [(i, lax.rem(j + k, ngy)) for k in range(1, ngy)]
        peers = ups + downs + [core_peer, inner_peer] + outer_peers + gy_peers

        fetch = pltpu.make_async_copy(weight_hbm, weight, s_fetch)
        fetch.start()
        barrier = pltpu.get_barrier_semaphore()
        for peer in peers:
            pl.semaphore_signal(barrier, inc=1, device_id=peer, device_id_type=MESH)

        live = [valid[0, 0, s] for s in range(bricks)]
        live_f = [v.astype(F32) for v in live]
        for s in range(bricks):
            ge[s * 64 : (s + 1) * 64] = (cot[0, 0, s].astype(F32) * live_f[s]).astype(BF)
        own = ge[0:rows]
        gface[...] = dot(picks[0 : 2 * frows], own).astype(BF)
        pl.semaphore_wait(barrier, len(peers))

        def remote(src, dst, ssem, rsem, peer):
            return pltpu.make_async_remote_copy(
                src_ref=src, dst_ref=dst, send_sem=ssem, recv_sem=rsem,
                device_id=peer, device_id_type=MESH,
            )

        face_copies = []
        for c in range(3):
            src = gface.at[pl.ds(frows * (c % 2), frows)]
            dst = ge.at[pl.ds(rows + c * frows, frows)]
            copy = remote(src, dst, s_g.at[c], r_g.at[c], downs[c])
            copy.start()
            face_copies.append(copy)

        for s in range(bricks):
            moved = dot_nt(perm[...], feat[0, 0, s]) * live_f[s]
            for cls in range(8):
                x_ref[cls, s * 64 : (s + 1) * 64] = moved[cls * 64 : (cls + 1) * 64].astype(BF)
        for cls in range(8):
            xt_ref[cls] = dot_nt(eye[...], x_ref[cls]).astype(BF)

        groups = 8 * bricks
        row_id = lax.broadcasted_iota(jnp.int32, (4 * groups, 128), 0)
        lane_id = lax.broadcasted_iota(jnp.int32, (4 * groups, 128), 1)
        counts = jnp.zeros((4 * groups, 128), F32)

        def count(total, kind, source, target, code):
            at = jnp.where(target < bricks, kind * groups + 8 * target + code, -1)
            return total + jnp.where((row_id == at) & (lane_id == source), 1.0, 0.0)

        for e in range(local_count):
            counts = count(counts, 0, lrules[0, 0, 0, e], lrules[0, 0, 1, e], lcodes[0, 0, e])
        for c in range(3):
            for e in range(remote_count):
                counts = count(
                    counts, c + 1, rrules[0, 0, c, 0, e], rrules[0, 0, c, 1, e], rcodes[0, c, 0, e]
                )
        spread = dot(counts.astype(BF), slot_of[...])

        for d in range(8):
            codes = [k for k in range(8) if k & ~d == 0]
            full = {k: blocks[PAIR_AT[(d, k)]].astype(F32) for k in codes}
            for kind in range(4):
                need = (0, 1, 2, 3)[kind]
                lo, hi = ((0, 64), (0, 16), (64, 80), (0, 16))[kind]
                for t in range(bricks):
                    total = jnp.zeros((hi - lo, rows), F32)
                    for k in codes:
                        if k & need == need:
                            at = kind * groups + 8 * t + k
                            total = total + spread[at : at + 1] * full[k][lo:hi]
                    first = t * 64 if kind == 0 else rows + (kind - 1) * frows + t * 16
                    m_ref[d, first : first + hi - lo] = total.astype(BF)

        for copy in face_copies:
            copy.wait()
        grads = dot(ge[...], twice[...]).astype(BF)
        for d in range(8):
            g_ref[d] = dot_tn(m_ref[d], grads).astype(BF)

        a_copies = []
        built = 0
        first_lanes = lax.broadcasted_iota(jnp.int32, (right, half), 1) < channels - half
        for tap, cls, shift in TAPS:
            wg[tap * channels : (tap + 1) * channels] = dot(xt_ref[cls], g_ref[shift])
            while built < chips and 2 * share * (built + 1) <= (tap + 1) * channels:
                for h in range(2):
                    first = share * (2 * built + h)
                    block = wg[first : first + share, 0:half].astype(BF)
                    tail = wg[first : first + share, half:wide]
                    fill = jnp.zeros((left - share, half), BF)
                    buf[2 * built + h, 0:left] = jnp.concatenate([block, fill], axis=0)
                    rest = jnp.zeros((2 * right - share, half), F32)
                    later = jnp.concatenate([tail[right:share], rest], axis=0)
                    packed = jnp.where(first_lanes, tail[0:right], later)
                    buf[2 * built + h, left:padded] = packed.astype(BF)
                copy = remote(
                    buf.at[2 * built + 1 - core], recv_a.at[built],
                    s_a.at[built], r_a.at[built], core_peer,
                )
                copy.start()
                a_copies.append(copy)
                built += 1

        fetch.wait()
        for tap in range(27):
            w_ref[tap] = weight[:, tap * channels : (tap + 1) * channels]

        def forward(d):
            total = None
            for tap, cls, shift in TAPS:
                if shift == d:
                    term = dot_nt(x_ref[cls], w_ref[tap])
                    total = term if total is None else total + term
            t_ref[d] = total

        for copy in a_copies:
            copy.wait_recv()

        def core_sum(m, lo, n):
            mine = buf[2 * m + core, lo : lo + n].astype(F32)
            return (mine + recv_a[m, lo : lo + n].astype(F32)).astype(BF)

        x_copies, b_copies = [], []
        for q in range(max(nq, np_)):
            if q < np_:
                lo, n = parts[q]
                for m in range(chips):
                    for g in range(ngy):
                        xacc[g, m % 2, m // 2, lo : lo + n] = core_sum(m, base + g * part + lo, n)
                started = []
                for k in range(1, ngy):
                    copy = remote(
                        xacc.at[lax.rem(j + k, ngy), :, :, pl.ds(lo, n)],
                        recv_x.at[k - 1, :, :, pl.ds(lo, n)],
                        s_x.at[q, k - 1], r_x.at[q, k - 1], gy_peers[k - 1],
                    )
                    copy.start()
                    started.append(copy)
                x_copies.append(started)
            if q < nq:
                lo, n = chunks[q]
                for m in range(chips):
                    acc[m % 2, m // 2, lo : lo + n] = core_sum(m, lo, n)
                copy = remote(
                    acc.at[1 - inner, :, pl.ds(lo, n)], recv_b.at[:, pl.ds(lo, n)],
                    s_b.at[q], r_b.at[q], inner_peer,
                )
                copy.start()
                b_copies.append(copy)

        for d in range(8):
            forward(d)

        total = None
        for d in range(8):
            value = t_ref[d]
            high = value.astype(BF)
            low = (value - high.astype(F32)).astype(BF)
            term = dot(m_ref[d], high) + dot(m_ref[d], low)
            total = term if total is None else total + term
        totals[...] = total[0:rows]
        fsend[...] = total[rows:ext].astype(BF)
        f_copies = []
        for c in range(3):
            span = pl.ds(c * frows, frows)
            copy = remote(fsend.at[span], frecv.at[span], s_f.at[c], r_f.at[c], ups[c])
            copy.start()
            f_copies.append(copy)

        def second(q):
            lo, n = chunks[q]
            b_copies[q].wait_recv()
            for o in range(outer):
                acc2[o, lo : lo + n] = (
                    acc[inner, o, lo : lo + n].astype(F32) + recv_b[o, lo : lo + n].astype(F32)
                ).astype(BF)
            started = []
            for k in range(1, outer):
                copy = remote(
                    acc2.at[lax.rem(z + k, outer), pl.ds(lo, n)], recv_c.at[k - 1, pl.ds(lo, n)],
                    s_c.at[q, k - 1], r_c.at[q, k - 1], outer_peers[k - 1],
                )
                copy.start()
                started.append(copy)
            return started

        def third(q):
            lo, n = chunks[q]
            total = acc2[z, lo : lo + n].astype(F32)
            for k in range(1, outer):
                c_copies[q][k - 1].wait_recv()
                total = total + recv_c[k - 1, lo : lo + n].astype(F32)
            final[j, lo : lo + n] = total.astype(BF)
            started = []
            for k in range(1, ngy):
                mine = final.at[j, pl.ds(lo, n)]
                copy = remote(mine, mine, s_d.at[q, k - 1], r_d.at[q, k - 1], gy_peers[k - 1])
                copy.start()
                started.append(copy)
            return started

        def part_x(q):
            lo, n = parts[q]
            for copy in x_copies[q]:
                copy.wait_recv()
            for h in range(2):
                for o in range(outer):
                    total = xacc[j, h, o, lo : lo + n].astype(F32)
                    for k in range(1, ngy):
                        total = total + recv_x[k - 1, h, o, lo : lo + n].astype(F32)
                    yacc[h, o, lo : lo + n] = total.astype(BF)
            copy = remote(
                yacc.at[1 - inner, :, pl.ds(lo, n)], recv_y.at[:, pl.ds(lo, n)],
                s_y.at[q], r_y.at[q], inner_peer,
            )
            copy.start()
            return copy

        def part_y(q):
            lo, n = parts[q]
            y_copies[q].wait_recv()
            for o in range(outer):
                zacc[o, lo : lo + n] = (
                    yacc[inner, o, lo : lo + n].astype(F32) + recv_y[o, lo : lo + n].astype(F32)
                ).astype(BF)
            started = []
            for k in range(1, outer):
                copy = remote(
                    zacc.at[lax.rem(z + k, outer), pl.ds(lo, n)], recv_z.at[k - 1, pl.ds(lo, n)],
                    s_z.at[q, k - 1], r_z.at[q, k - 1], outer_peers[k - 1],
                )
                copy.start()
                started.append(copy)
            return started

        def part_z(q):
            lo, n = parts[q]
            total = zacc[z, lo : lo + n].astype(F32)
            for k in range(1, outer):
                z_copies[q][k - 1].wait_recv()
                total = total + recv_z[k - 1, lo : lo + n].astype(F32)
            gathered[j, lo : lo + n] = total
            started = []
            for k in range(1, ngy):
                mine = gathered.at[j, pl.ds(lo, n)]
                copy = remote(mine, mine, s_w.at[q, k - 1], r_w.at[q, k - 1], gy_peers[k - 1])
                copy.start()
                started.append(copy)
            return started

        def feature_class(cls):
            total = None
            for tap, tap_cls, shift in TAPS:
                if tap_cls == cls:
                    term = dot(g_ref[shift, :, 0:channels], w_ref[tap])
                    total = term if total is None else total + term
            for s in range(bricks):
                fcls[s, cls * 64 : (cls + 1) * 64] = (
                    total[s * 64 : (s + 1) * 64] * live_f[s]
                ).astype(BF)

        c_copies, d_copies, y_copies, z_copies, w_copies = [], [], [], [], []
        feature_class(0)
        feature_class(1)
        for q in range(max(nq, np_)):
            if q < nq:
                c_copies.append(second(q))
            if q < np_:
                y_copies.append(part_x(q))
            for cls in (2, 3, 4) if q == 0 else (5, 6) if q == 1 else ():
                feature_class(cls)
        for cls in range(5, 8) if max(nq, np_) == 1 else (7,):
            feature_class(cls)
        for q in range(max(nq, np_)):
            if q < np_:
                z_copies.append(part_y(q))
            if q == 0:
                for s in range(bricks):
                    fgrad[0, 0, s] = dot_tn(fcls[s], perm[...]).astype(BF)
            if q < nq:
                d_copies.append(third(q))
        for copy in f_copies:
            copy.wait()
        result = totals[...] + dot(picks_t[...], frecv[...])
        for s in range(bricks):
            out[0, 0, s] = (result[s * 64 : (s + 1) * 64] * live_f[s]).astype(BF)
        for q in range(np_):
            w_copies.append(part_z(q))

        for q, (lo, n) in enumerate(chunks):
            for copy in d_copies[q]:
                copy.wait_recv()
            total = final[0, lo : lo + n].astype(F32)
            for k in range(1, ngy):
                total = total + final[k, lo : lo + n].astype(F32)
            summed[lo : lo + n] = total
        for copies in w_copies:
            for copy in copies:
                copy.wait_recv()
        for g in range(ngy):
            summed[base + g * part : base + (g + 1) * part] = gathered[g]
        wgrad[0:half] = jnp.transpose(summed[0:left])[:, 0:share]
        turned = jnp.transpose(summed[left:padded])
        tail = channels - half
        wgrad[half:channels, 0:right] = turned[0:tail]
        wgrad[half:channels, right:share] = turned[tail : 2 * tail, 0 : share - right]

        for copy in a_copies + b_copies + y_copies:
            copy.wait_send()
        for copies in c_copies + d_copies + x_copies + z_copies + w_copies:
            for copy in copies:
                copy.wait_send()

    dma = pltpu.SemaphoreType.DMA
    scratch = [
        pltpu.VMEM((channels, 27 * channels), BF),
        pltpu.VMEM((27, channels, channels), BF),
        pltpu.VMEM((8, rows, channels), BF),
        pltpu.VMEM((8, channels, rows), BF),
        pltpu.VMEM((8, ext, rows), BF),
        pltpu.VMEM((8, rows, wide), BF),
        pltpu.VMEM((8, rows, channels), F32),
        pltpu.VMEM((ext, channels), BF),
        pltpu.VMEM((2 * frows, channels), BF),
        pltpu.VMEM((3 * frows, channels), BF),
        pltpu.VMEM((3 * frows, channels), BF),
        pltpu.VMEM((rows, channels), F32),
        pltpu.VMEM((bricks, 512, channels), BF),
        pltpu.VMEM((27 * channels, wide), F32),
        pltpu.VMEM((ngx, padded, half), BF),
        pltpu.VMEM((chips, padded, half), BF),
        pltpu.VMEM((2, outer, base, half), BF),
        pltpu.VMEM((outer, base, half), BF),
        pltpu.VMEM((outer, base, half), BF),
        pltpu.VMEM((outer - 1, base, half), BF),
        pltpu.VMEM((ngy, base, half), BF),
        pltpu.VMEM((padded, half), F32),
        pltpu.VMEM((ngy, 2, outer, part, half), BF),
        pltpu.VMEM((ngy - 1, 2, outer, part, half), BF),
        pltpu.VMEM((2, outer, part, half), BF),
        pltpu.VMEM((outer, part, half), BF),
        pltpu.VMEM((outer, part, half), BF),
        pltpu.VMEM((outer - 1, part, half), BF),
        pltpu.VMEM((ngy, part, half), F32),
        dma((3,)), dma((3,)), dma((3,)), dma((3,)),
        dma((chips,)), dma((chips,)), dma((nq,)), dma((nq,)),
        dma((nq, outer - 1)), dma((nq, outer - 1)),
        dma((nq, ngy - 1)), dma((nq, ngy - 1)),
        dma((np_, ngy - 1)), dma((np_, ngy - 1)), dma((np_,)), dma((np_,)),
        dma((np_, outer - 1)), dma((np_, outer - 1)), dma((np_, ngy - 1)), dma((np_, ngy - 1)),
        dma,
    ]
    return kernel, scratch, share


def hand_over(a, b, c, a_out, b_out, c_out, sems):
    pairs = ((a, a_out), (b, b_out), (c, c_out))
    copies = [pltpu.make_async_copy(src, dst, sems.at[at]) for at, (src, dst) in enumerate(pairs)]
    for copy in copies:
        copy.start()
    for copy in copies:
        copy.wait()


def solution(mesh):
    ngx, ngy = mesh.shape["gx"], mesh.shape["gy"]

    def shards(
        features, weight, cotangent, valid, local_rules, local_codes, remote_rules, remote_codes
    ):
        bricks = features.shape[2]
        channels = features.shape[-1]
        local_count = local_codes.shape[-1]
        remote_count = remote_codes.shape[-1]
        kernel, scratch, share = make_kernel(
            ngx, ngy, bricks, local_count, remote_count, channels, 2
        )
        order = parity_order()
        perm = np.zeros((512, 512), np.float32)
        perm[np.arange(512), order] = 1
        picks = face_picks(bricks)
        slot_of = (np.arange(128)[:, None] == (np.arange(bricks * 64) // 64)[None, :]).astype(
            np.float32
        )
        twice = np.zeros((channels, 256), np.float32)
        twice[np.arange(channels), np.arange(channels)] = 1
        twice[np.arange(128, channels), np.arange(128, channels) + channels - 128] = 1
        consts = [
            jnp.asarray(c, BF)
            for c in (
                rule_blocks(bricks), perm, picks, picks.T, slot_of,
                np.eye(channels, dtype=np.float32), twice,
            )
        ]
        vmem = pl.BlockSpec(memory_space=pltpu.VMEM)
        anywhere = pl.BlockSpec(memory_space=pl.ANY)
        hbm = pl.BlockSpec(memory_space=pltpu.HBM)
        smem = pl.BlockSpec(memory_space=pltpu.SMEM)
        out, fgrad, wgrad = pl.pallas_call(
            kernel,
            out_shape=(
                jax.ShapeDtypeStruct(cotangent.shape, BF),
                jax.ShapeDtypeStruct((1, 1, bricks, channels, 512), BF),
                jax.ShapeDtypeStruct((channels, share), F32),
            ),
            in_specs=[smem] * 5 + [vmem, anywhere] + [vmem] * 8,
            out_specs=(vmem, vmem, vmem),
            scratch_shapes=scratch,
            compiler_params=pltpu.CompilerParams(
                collective_id=0, has_side_effects=True, vmem_limit_bytes=56 * 1024 * 1024
            ),
        )(
            valid, local_rules, local_codes, jnp.swapaxes(remote_rules, 2, 3),
            jnp.swapaxes(remote_codes, 1, 2), jnp.swapaxes(features, 3, 4), weight.T,
            cotangent, *consts,
        )
        out, fgrad, wgrad = pl.pallas_call(
            hand_over,
            out_shape=tuple(jax.ShapeDtypeStruct(a.shape, a.dtype) for a in (out, fgrad, wgrad)),
            in_specs=[vmem] * 3,
            out_specs=(hbm,) * 3,
            scratch_shapes=[pltpu.SemaphoreType.DMA((3,))],
        )(out, fgrad, wgrad)
        return out, jnp.swapaxes(fgrad, 3, 4), wgrad.T

    return jax.shard_map(
        shards,
        mesh=mesh,
        in_specs=(
            P("gx", "gy", None, None, None),
            P(),
            P("gx", "gy", None, None, None),
            P("gx", "gy", None),
            P("gx", "gy", None, None),
            P("gx", "gy", None),
            P("gx", "gy", None, None, None),
            P("gx", "gy", None, None),
        ),
        out_specs=(P("gx", "gy", None, None, None), P("gx", "gy", None, None, None), P("gx", None)),
        check_vma=False,
    )
```
